128 devices in a mesh: expert: 8 (over z, y_lo), tensor: 16 (over y_hi, x, core).
Axes of the slice: x: 4, y: 4 (y_hi: 2, y_lo: 2; y = y_hi * 2 + y_lo), z: 4, core: 2. Of those that a mesh axis runs over, the one named last changes fastest.
Arguments:
- tokens: bfloat16 [2048, 3072], P('expert'), may hold values from -6 to 6
- cotangent: bfloat16 [2048, 3072], P('expert'), may hold values from -6 to 6
- expert_ids: int32 [2048, 2], P('expert'), may hold values from 0 to 7, all different within a row; in each aligned block of 256 rows (0 to 255, 256 to 511, ...) at most 96 rows name the same one
- gates: float32 [2048, 2], P('expert'), may hold values from 0.1 to 1
- w_gate: bfloat16 [8, 3072, 8192], P('expert', None, 'tensor'), may hold values from -0.109375 to 0.109375
- w_up: bfloat16 [8, 3072, 8192], P('expert', None, 'tensor'), may hold values from -0.109375 to 0.109375
- w_down: bfloat16 [8, 8192, 3072], P('expert', 'tensor'), may hold values from -0.0625 to 0.0625
Outputs:
- mixed: bfloat16 [2048, 3072], P('expert')
- token_grad: bfloat16 [2048, 3072], P('expert')
- grad_gate: bfloat16 [8, 3072, 8192], P('expert', None, 'tensor')
- grad_up: bfloat16 [8, 3072, 8192], P('expert', None, 'tensor')
- grad_down: bfloat16 [8, 8192, 3072], P('expert', 'tensor')
The draws below stay inside these ranges and needn't reach their ends.
Inputs may be any that keep to these rules, and one draw needn't show every extreme that they name: `expert_ids`: each token names two different experts. In one block of 256 rows no expert is named more than 96 times, and in every draw some block names some expert exactly 96 times.
All inputs are finite; a program needn't handle non-finite values.
Results may differ from the reference program's by a relative error of at most 0.02.
Values may be sent and summed in bfloat16 or wider, within the bound.
No kernel may reach another device: no remote copies, remote signals or barrier semaphores. Data moves between devices by JAX's collectives and lax.ppermute only.
A program may use at most 128 MiB of HBM per device.

```python
import math
import jax
import jax.numpy as jnp
import numpy as np
from jax import lax

D = 3072
FF = 8192
TOK_DEV = 256
EXPERTS = 8
CAP = 96
TOKENS = 2048
N_TENSOR = 16


def block_levels(key, extent, pieces, least, largest):
    level = 1.0
    for dim, shards_of in pieces:
        steps = jax.random.uniform(jax.random.fold_in(jax.random.fold_in(key, 6), dim), (shards_of,), jnp.float32, least / len(pieces), largest / len(pieces))
        level = level * jnp.repeat(jnp.exp(steps), extent[dim] // shards_of).reshape((-1,) + (1,) * (len(extent) - 1 - dim))
    return level


def shared_out(rng, own, number, rows, number_of, top, bound, slope):
    sequence = jax.random.permutation(rng, number_of)
    packed, usual = shares(number_of, rows * top, bound, slope, True), shares(number_of, rows * top, bound, slope, False)
    places = jnp.arange(number_of)

    def named(lengths, offset_by):
        used = int((lengths > 0).sum())
        fixed = max(1, used // 4)
        shifted = fixed + (places - fixed + offset_by * (used - fixed)) % max(1, number_of - fixed)
        return jnp.zeros((number_of,), jnp.int32).at[sequence[jnp.where(places < fixed, places, shifted)]].set(jnp.asarray(lengths, jnp.int32))

    lengths = jnp.where(number % 4 == 0, named(packed, number // 4), named(usual, number - number // 4 - 1))
    mixed = jax.random.permutation(jax.random.fold_in(own, 3), number_of)
    donor, sink = mixed[0:number_of // 2 * 2:2], mixed[1:number_of // 2 * 2:2]
    slack = jnp.minimum(lengths[donor] - 1, bound - lengths[sink]) // 2
    slack = jnp.where((donor == sequence[0]) | (sink == sequence[0]) | (lengths[sink] == 0), 0, jnp.maximum(slack, 0))
    shifted = jax.random.randint(jax.random.fold_in(own, 4), (number_of // 2,), 0, 1 << 20) % (slack + 1)
    lengths = lengths.at[donor].add(-shifted).at[sink].add(shifted)
    labels = jnp.searchsorted(jnp.cumsum(lengths), jnp.arange(rows * top), side="right").astype(jnp.int32)
    table = labels.reshape(top, rows).T
    table = table[jax.random.permutation(jax.random.fold_in(own, 1), rows)]
    offset_by = jax.random.randint(jax.random.fold_in(own, 2), (rows, 1), 0, top)
    return jnp.take_along_axis(table, (jnp.arange(top)[None, :] + offset_by) % top, axis=1)


def shares(amount, total, reach, slope, full):
    portions = [(1 << 20) // math.isqrt(rank ** slope) + 1 for rank in range(1, amount + 1)]
    largest = reach if full else min(reach, max(-(-total // amount), total * portions[0] // sum(portions)))
    least = 1 if total - largest >= amount - 1 else 0
    given, rest = [largest] + [least] * (amount - 1), total - largest - least * (amount - 1)
    while rest > 0:
        candidates = [i for i in range(1, amount) if given[i] < largest] or [i for i in range(1, amount) if given[i] < reach]
        whole, left = sum([portions[i] for i in candidates]), rest
        for i in candidates:
            extra = min(reach - given[i], max(1, left * portions[i] // whole), rest)
            given[i] = given[i] + extra
            rest = rest - extra
    return np.array(given)


def gaussian(own_key, dims, spread, reach, cuts=(), kind=jnp.bfloat16):
    entries = spread * jax.random.normal(own_key, dims, jnp.float32)
    if cuts:
        entries = entries * block_levels(own_key, dims, cuts, -0.22, 0.18)
    return jnp.clip(entries, -reach, reach).astype(kind)


def setup_inputs(seed: int = 0) -> dict:
    seeds = jax.random.split(jax.random.key(seed), 8)
    tokens = gaussian(seeds[0], (TOKENS, D), 1.0, 6.0, ((0, 8),))
    cotangent = gaussian(seeds[1], (TOKENS, D), 1.0, 6.0, ((0, 8),))
    expert_ids_keys = jax.random.split(jax.random.fold_in(seeds[2], 1), TOKENS // TOK_DEV)
    expert_ids_turns = jax.random.permutation(jax.random.fold_in(seeds[2], 3), TOKENS // TOK_DEV)
    expert_ids = jax.vmap(lambda own, number: shared_out(jax.random.fold_in(seeds[2], 2), own, number, TOK_DEV, EXPERTS, 2, CAP, 2))(expert_ids_keys, expert_ids_turns).reshape((TOKENS, 2))
    gates = jnp.clip(0.1 + 0.9 * jax.random.uniform(seeds[3], (TOKENS, 2), jnp.float32) ** block_levels(seeds[3], (TOKENS, 2), ((0, 8),), -0.2, 0.2), 0.1, 1.0)
    w_gate = gaussian(seeds[4], (EXPERTS, D, FF), D ** -0.5, 0.109375, ((0, 8), (2, 16)))
    w_up = gaussian(seeds[5], (EXPERTS, D, FF), D ** -0.5, 0.109375, ((0, 8), (2, 16)))
    w_down = gaussian(seeds[6], (EXPERTS, FF, D), FF ** -0.5, 0.0625, ((0, 8), (1, 16)))
    return dict(tokens=tokens, cotangent=cotangent, expert_ids=expert_ids, gates=gates, w_gate=w_gate, w_up=w_up, w_down=w_down)


def block_sum(left_set, right_set, row_count):
    def add_block(running, pair_blocks):
        lefts, rights = pair_blocks
        product = jnp.dot(lefts[0], rights[0], preferred_element_type=jnp.float32)
        for position in range(1, len(lefts)):
            product = product + jnp.dot(lefts[position], rights[position], preferred_element_type=jnp.float32)
        rounded = lax.optimization_barrier(product.astype(jnp.bfloat16))
        return running + rounded.astype(jnp.float32), None

    start_sum = jnp.zeros((row_count, D), jnp.float32)
    running, ignored = lax.scan(add_block, start_sum, (left_set, right_set))
    return running.astype(jnp.bfloat16)


def reference(tokens, cotangent, expert_ids, gates, w_gate, w_up, w_down):
    blocks = TOKENS // TOK_DEV
    slot_total = blocks * CAP
    shard_size = FF // N_TENSOR
    per_block = expert_ids.reshape(blocks, TOK_DEV * 2)
    onehot = (per_block[:, :, None] == jnp.arange(EXPERTS, dtype=jnp.int32)[None, None, :]).astype(jnp.int32)
    before = jnp.cumsum(onehot, axis=1) - onehot
    ranked = jnp.sum(before * onehot, axis=2)
    row_index = (jnp.arange(blocks, dtype=jnp.int32)[:, None] * CAP + ranked).reshape(TOKENS, 2).astype(jnp.int32)
    scaled = (gates[:, :, None] * cotangent[:, None, :].astype(jnp.float32)).astype(jnp.bfloat16)
    mixed_sum = jnp.zeros((TOKENS, D), jnp.float32)
    grad_sum = jnp.zeros((TOKENS, D), jnp.float32)
    gate_grads = []
    up_grads = []
    down_grads = []
    for expert in range(EXPERTS):
        chosen = expert_ids == expert
        target = jnp.where(chosen, row_index, slot_total).astype(jnp.int32)
        routed = jnp.zeros((slot_total, D), jnp.bfloat16)
        d_routed = jnp.zeros((slot_total, D), jnp.bfloat16)
        for column in range(2):
            routed = routed.at[target[:, column]].set(tokens, mode="drop")
            d_routed = d_routed.at[target[:, column]].set(scaled[:, column], mode="drop")
        gate_act = jnp.dot(routed, w_gate[expert], preferred_element_type=jnp.float32)
        up_act = jnp.dot(routed, w_up[expert], preferred_element_type=jnp.float32)
        squashed = jax.nn.sigmoid(gate_act)
        silu_act = gate_act * squashed
        hidden = (silu_act * up_act).astype(jnp.bfloat16)
        hidden_blocks = hidden.reshape(slot_total, N_TENSOR, shard_size).transpose(1, 0, 2)
        down_blocks = w_down[expert].reshape(N_TENSOR, shard_size, D)
        expert_out = block_sum((hidden_blocks,), (down_blocks,), slot_total)
        d_hidden = lax.dot_general(d_routed, w_down[expert], (((1,), (1,)), ((), ())), preferred_element_type=jnp.float32)
        down_grads.append(lax.dot_general(hidden, d_routed, (((0,), (0,)), ((), ())), preferred_element_type=jnp.float32).astype(jnp.bfloat16))
        d_up = (d_hidden * silu_act).astype(jnp.bfloat16)
        d_gate = (d_hidden * up_act * squashed * (1.0 + gate_act * (1.0 - squashed))).astype(jnp.bfloat16)
        gate_grads.append(lax.dot_general(routed, d_gate, (((0,), (0,)), ((), ())), preferred_element_type=jnp.float32).astype(jnp.bfloat16))
        up_grads.append(lax.dot_general(routed, d_up, (((0,), (0,)), ((), ())), preferred_element_type=jnp.float32).astype(jnp.bfloat16))
        d_gate_blocks = d_gate.reshape(slot_total, N_TENSOR, shard_size).transpose(1, 0, 2)
        d_up_blocks = d_up.reshape(slot_total, N_TENSOR, shard_size).transpose(1, 0, 2)
        gate_rows = w_gate[expert].reshape(D, N_TENSOR, shard_size).transpose(1, 2, 0)
        up_rows = w_up[expert].reshape(D, N_TENSOR, shard_size).transpose(1, 2, 0)
        d_input = block_sum((d_gate_blocks, d_up_blocks), (gate_rows, up_rows), slot_total)
        for column in range(2):
            fetch_rows = jnp.where(chosen[:, column], row_index[:, column], 0).astype(jnp.int32)
            taken_mask = chosen[:, column][:, None]
            taken_out = jnp.take(expert_out, fetch_rows, axis=0).astype(jnp.float32)
            taken_grad = jnp.take(d_input, fetch_rows, axis=0).astype(jnp.float32)
            mixed_sum = mixed_sum + jnp.where(taken_mask, gates[:, column][:, None] * taken_out, 0.0)
            grad_sum = grad_sum + jnp.where(taken_mask, taken_grad, 0.0)
    return (mixed_sum.astype(jnp.bfloat16), grad_sum.astype(jnp.bfloat16), jnp.stack(gate_grads), jnp.stack(up_grads), jnp.stack(down_grads))
```

```python
import jax
import jax.numpy as jnp
from jax import lax
from jax.experimental import pallas as pl
from jax.experimental.pallas import tpu as pltpu
from jax.sharding import Mesh, PartitionSpec as P

F32, BF16 = jnp.float32, jnp.bfloat16
EXP = ("z", "yl")
TEN = ("yh", "x", "c")
NN = (((1,), (0,)), ((), ()))
NT = (((1,), (1,)), ((), ()))
TN = (((0,), (0,)), ((), ()))


def mm(a, b, dims=NN):
    return lax.dot_general(a, b, dims, preferred_element_type=F32)


def call(kernel, out_shape, grid, in_specs, out_specs, scratch=(), mib=24):
    return pl.pallas_call(
        kernel,
        out_shape=out_shape,
        grid_spec=pltpu.PrefetchScalarGridSpec(
            num_scalar_prefetch=1,
            grid=grid,
            in_specs=in_specs,
            out_specs=out_specs,
            scratch_shapes=list(scratch),
        ),
        compiler_params=pltpu.CompilerParams(vmem_limit_bytes=mib * 2**20),
    )


def shape(*dims, dtype=BF16):
    return jax.ShapeDtypeStruct(dims, dtype)


def in_hbm(*values):
    return [pltpu.with_memory_space_constraint(v, pltpu.HBM) for v in values]


def block(dims, index=None):
    return pl.BlockSpec(
        dims, index or (lambda *_: (0,) * len(dims)), pipeline_mode=pl.Buffered(1)
    )


def chunk_index(s, j):
    core = s[0] if j < 4 else 1 - s[0]
    return core * 4 + lax.rem(s[1] + j % 4, 4)


def to_index(s, r):
    return ((s[2] + r // 2) & 3) * 2 + (s[3] ^ (r % 2))


def from_index(s, r):
    return ((s[2] + 4 - r // 2) & 3) * 2 + (s[3] ^ (r % 2))


def route(scal, ids, gates, tokens, cotangent, experts, cap):
    toks, features = tokens.shape
    half, part, slots = features // 2, features // 8, experts * cap

    def kernel(s, ids_ref, gates_ref, tok_ref, cot_ref, *outs):
        rows = outs[-1]
        ids_here = jnp.transpose(ids_ref[...])
        named0, named1 = ids_here[:, 0:1], ids_here[:, 1:2]
        lane = lax.broadcasted_iota(jnp.int32, (toks, 128), 1)
        named = ((named0 == lane) | (named1 == lane)).astype(F32).astype(BF16)
        row = lax.broadcasted_iota(jnp.int32, (toks, toks), 0)
        col = lax.broadcasted_iota(jnp.int32, (toks, toks), 1)
        earlier = (col < row).astype(F32).astype(BF16)
        count = mm(earlier, named).astype(BF16)
        ex = lax.broadcasted_iota(jnp.int32, (128, slots), 0) * cap
        at = lax.broadcasted_iota(jnp.int32, (128, slots), 1)
        spread = ((at >= ex) & (at < ex + cap)).astype(F32).astype(BF16)
        rank = mm(count, spread)
        slot = lax.broadcasted_iota(jnp.int32, (toks, slots), 1)
        first, second = named0 * cap, named1 * cap
        in0 = (slot >= first) & (slot < first + cap)
        in1 = (slot >= second) & (slot < second + cap)
        base = jnp.where(in0, first, jnp.where(in1, second, -4 * slots))
        hit = rank.astype(jnp.int32) + base == slot
        g = jnp.transpose(gates_ref[...])
        weight = jnp.where(hit, jnp.where(in0, g[:, 0:1], g[:, 1:2]), 0.0)
        placing = hit.astype(F32).astype(BF16)
        hi = weight.astype(BF16)
        lo = (weight - hi.astype(F32)).astype(BF16)
        outs[9][...] = placing
        outs[10][...] = hi
        outs[11][...] = lo
        cot = cot_ref[...]
        outs[8][...] = (mm(hi, cot, TN) + mm(lo, cot, TN)).astype(BF16)
        rows[...] = mm(placing, tok_ref[...], TN).astype(BF16)
        for r in range(experts):
            at = pl.multiple_of(to_index(s, r) * cap, cap)
            outs[r][...] = rows[pl.ds(at, cap)]

    out = call(
        kernel,
        [pltpu.HBM((cap, half), BF16)] * 8 + [shape(slots, part)] + [shape(toks, slots)] * 3,
        (1,),
        [
            block(ids.shape[::-1]),
            block(gates.shape[::-1]),
            block((toks, half), lambda k, s: (0, s[0])),
            block((toks, part), lambda k, s: (0, s[0] * 4 + s[1])),
        ],
        [block((cap, half))] * 8 + [block((slots, part))] + [block((toks, slots))] * 3,
        [pltpu.VMEM((slots, half), BF16)],
    )(scal, ids.T, gates.T, *in_hbm(tokens, cotangent))
    return out[:8], out[8], out[9], out[10], out[11]


def gate_up(scal, own, oth, wg, wu):
    cap, half = own[0].shape
    rows, ff, tiles = 8 * cap, wg.shape[1], 2
    tile, kb = rows // tiles, wg.shape[0] // 4

    def kernel(s, *refs):
        own_refs, oth_refs, (wg_ref, wu_ref) = refs[:8], refs[8:16], refs[16:18]
        hid_ref, a_ref, b_ref, all_ref, wg_v, wu_v, sem, wsem = refs[18:]
        copies, wcopies = [], []
        for k in range(4):
            here = pl.ds(k * kb, kb)
            wcopies.append(pltpu.make_async_copy(wg_ref.at[here], wg_v.at[here], wsem.at[2 * k]))
            wcopies.append(
                pltpu.make_async_copy(wu_ref.at[here], wu_v.at[here], wsem.at[2 * k + 1])
            )
        for r in range(8):
            at = pl.ds(pl.multiple_of(from_index(s, r) * cap, cap), cap)
            for side, ref in ((0, own_refs[r]), (1, oth_refs[r])):
                core = s[0] if side == 0 else 1 - s[0]
                lanes = pl.ds(pl.multiple_of(core * half, 256), half)
                copies.append(
                    pltpu.make_async_copy(ref, all_ref.at[at, lanes], sem.at[2 * r + side])
                )
        for cp in copies + wcopies:
            cp.start()
        for cp in copies:
            cp.wait()
        for t in range(tiles):
            here = pl.ds(t * tile, tile)
            gate = up = None
            for k in range(4):
                if t == 0:
                    wcopies[2 * k].wait()
                    wcopies[2 * k + 1].wait()
                left = all_ref[here, pl.ds(k * kb, kb)]
                pg = mm(left, wg_v[pl.ds(k * kb, kb)])
                pu = mm(left, wu_v[pl.ds(k * kb, kb)])
                gate = pg if k == 0 else gate + pg
                up = pu if k == 0 else up + pu
            sig = jax.nn.sigmoid(gate)
            silu = gate * sig
            hid_ref[here] = (silu * up).astype(BF16)
            a_ref[here] = silu
            b_ref[here] = up * sig * (1.0 + gate * (1.0 - sig))

    anywhere = pl.BlockSpec(memory_space=pl.ANY)
    return call(
        kernel,
        [
            pltpu.VMEM((rows, ff), BF16),
            pltpu.VMEM((rows, ff), F32),
            pltpu.VMEM((rows, ff), F32),
            pltpu.HBM((rows, 2 * half), BF16),
        ],
        (1,),
        [anywhere] * 18,
        [block((rows, ff))] * 3 + [block((rows, 2 * half))],
        [
            pltpu.VMEM(wg.shape, BF16),
            pltpu.VMEM(wu.shape, BF16),
            pltpu.SemaphoreType.DMA((16,)),
            pltpu.SemaphoreType.DMA((8,)),
        ],
    )(scal, *in_hbm(*own, *oth, wg, wu))


def back_hidden(scal, chunks, wd, silu, dsilu):
    rows, cols = chunks[0].shape
    ff = wd.shape[0]

    def kernel(s, *refs):
        cr, (wd_ref, a_ref, b_ref, dgu_ref) = refs[:8], refs[8:]
        acc = None
        for j in range(8):
            at = pl.multiple_of(chunk_index(s, j) * cols, 128)
            part = mm(cr[j][...], wd_ref[:, pl.ds(at, cols)], NT)
            acc = part if acc is None else acc + part
        dgu_ref[:, :ff] = (acc * b_ref[...]).astype(BF16)
        dgu_ref[:, ff:] = (acc * a_ref[...]).astype(BF16)

    return call(
        kernel,
        pltpu.VMEM((rows, 2 * ff), BF16),
        (1,),
        [block((rows, cols))] * 8 + [block(wd.shape)] + [block((rows, ff))] * 2,
        block((rows, 2 * ff)),
    )(scal, *in_hbm(*chunks, wd), silu, dsilu)


def in_part(scal, d, mine, theirs, wg, wu, wg2, wu2):
    rows, ff = mine.shape[0], mine.shape[1] // 2
    cols = wg2.shape[0] // 4

    def kernel(s, m, t, w0, w1, w2, w3, out_ref):
        acc = mm(m[:, :ff], w0[...], NT) + mm(t[:, :ff], w2[...], NT)
        acc += mm(m[:, ff:], w1[...], NT) + mm(t[:, ff:], w3[...], NT)
        out_ref[...] = acc.astype(BF16)

    here = lambda k, s: (s[0] * 4 + lax.rem(s[1] + d, 4), 0)
    there = lambda k, s: (lax.rem(s[1] + d, 4), 0)
    return call(
        kernel,
        pltpu.HBM((rows, cols), BF16),
        (1,),
        [block((rows, 2 * ff))] * 2
        + [block((cols, ff), here)] * 2
        + [block((cols, ff), there)] * 2,
        block((rows, cols)),
        mib=16,
    )(scal, mine, theirs, *in_hbm(wg, wu, wg2, wu2))


def out_half(scal, hid, hid2, wd, wd2):
    rows, ff = hid.shape
    half = wd2.shape[1]
    cols = half // 2

    def kernel(s, h0, h1, w0, w1, out):
        out[...] = (mm(h0[...], w0[...]) + mm(h1[...], w1[...])).astype(BF16)

    return call(
        kernel,
        pltpu.HBM((rows, half), BF16),
        (2,),
        [
            block((rows, ff)),
            block((rows, ff)),
            pl.BlockSpec((ff, cols), lambda k, s: (0, s[0] * 2 + k)),
            pl.BlockSpec((ff, cols), lambda k, s: (0, k)),
        ],
        pl.BlockSpec((rows, cols), lambda k, s: (0, k)),
        mib=16,
    )(scal, hid, hid2, *in_hbm(wd, wd2))


def add(scal, *parts):
    rows, cols = parts[0].shape

    def kernel(s, *refs):
        acc = refs[0][...].astype(F32)
        for ref in refs[1:-1]:
            acc = acc + ref[...].astype(F32)
        refs[-1][...] = acc.astype(BF16)

    return call(
        kernel,
        shape(rows, cols),
        (1,),
        [block((rows, cols))] * len(parts),
        block((rows, cols)),
        mib=8,
    )(scal, *parts)


def combine(scal, mats, home, quarters):
    toks, slots = mats[0].shape
    cols = home.shape[1]
    n = len(mats)

    def kernel(s, *refs):
        mat_refs, home_ref, rest = refs[:n], refs[n], refs[n + 1 :]
        acc = mm(mat_refs[0][...], home_ref[...])
        for m in mat_refs[1:]:
            acc += mm(m[...], home_ref[...])
        if quarters:
            whole = rest[-1]
            whole[...] = acc
            for d in range(4):
                at = pl.multiple_of(lax.rem(s[1] + d, 4) * (cols // 4), 128)
                rest[d][...] = whole[:, pl.ds(at, cols // 4)].astype(BF16)
        else:
            rest[0][...] = acc.astype(BF16)

    if quarters:
        dims, k, extra = (toks, cols // 4), 4, [pltpu.VMEM((toks, cols), F32)]
    else:
        dims, k, extra = (toks, cols), 1, []
    return call(
        kernel,
        [shape(*dims)] * k,
        (1,),
        [block((toks, slots))] * n + [block((slots, cols))],
        [block(dims)] * k,
        extra,
        mib=12,
    )(scal, *mats, home)


def grad_in(scal, routed, dgu):
    rows, features = routed.shape
    ff = dgu.shape[1] // 2
    kb = features // 4

    def kernel(s, left_ref, dgu_ref, gg_ref, gu_ref):
        res = mm(left_ref[...], dgu_ref[...], TN).astype(BF16)
        gg_ref[...] = res[:, :ff]
        gu_ref[...] = res[:, ff:]

    return call(
        kernel,
        [pltpu.HBM((features, ff), BF16)] * 2,
        (4,),
        [pl.BlockSpec((rows, kb), lambda k, s: (0, k)), block(dgu.shape)],
        [pl.BlockSpec((kb, ff), lambda k, s: (k, 0))] * 2,
        mib=20,
    )(scal, *in_hbm(routed), dgu)


def grad_out(scal, hid, chunks):
    rows, cols = chunks[0].shape
    ff = hid.shape[1]

    def kernel(s, hid_ref, *refs):
        for j in range(8):
            at = pl.multiple_of(chunk_index(s, j) * cols, 128)
            refs[8][:, pl.ds(at, cols)] = mm(hid_ref[...], refs[j][...], TN).astype(BF16)

    return call(
        kernel,
        pltpu.HBM((ff, 8 * cols), BF16),
        (1,),
        [block((rows, ff))] + [block((rows, cols))] * 8,
        block((ff, 8 * cols)),
        mib=20,
    )(scal, hid, *in_hbm(*chunks))


def assemble(scal, chunks):
    rows, cols = chunks[0].shape

    def kernel(s, *refs):
        for j in range(8):
            at = pl.multiple_of(chunk_index(s, j) * cols, 128)
            refs[8][:, pl.ds(at, cols)] = refs[j][...]

    return call(
        kernel,
        shape(rows, 8 * cols),
        (1,),
        [block((rows, cols))] * 8,
        block((rows, 8 * cols)),
        mib=8,
    )(scal, *chunks)


def swap(v, axis="c"):
    return lax.ppermute(v, axis, [(0, 1), (1, 0)])


def shift(v, axis, d):
    n = lax.axis_size(axis)
    return lax.ppermute(v, axis, [(i, (i + d) % n) for i in range(n)])


def pairs(dz, dy):
    step = 0 if dy == 0 else 1 if dz % 2 == 0 else -1
    out = []
    for z in range(4):
        for y in range(4):
            to = (y + step) % 4
            out.append(
                ((z * 2 + y % 2) * 2 + y // 2, ((z + dz) % 4 * 2 + to % 2) * 2 + to // 2)
            )
    return out


def exchange(blocks):
    out = list(blocks)
    for r in (4, 5, 2, 3, 6, 7, 1):
        out[r] = lax.ppermute(blocks[r], ("z", "yl", "yh"), pairs(r // 2, r % 2))
    return out


def all_exchange(rows):
    cut = rows.reshape(8, rows.shape[0] // 8, rows.shape[1])
    return lax.all_to_all(cut, EXP, split_axis=0, concat_axis=0, tiled=True).reshape(rows.shape)


def gather_x(v):
    far, right, left = shift(v, "x", -2), shift(v, "x", -1), shift(v, "x", 1)
    return [v, right, far, left]


def after(value, *earlier):
    return lax.optimization_barrier((value, earlier))[0]


def finish(scal, mine):
    total = add(scal, mine, swap(mine, "yh"))
    chunks = gather_x(total)
    return assemble(scal, chunks + [swap(v) for v in chunks])


def on_device(tokens, cotangent, expert_ids, gates, w_gate, w_up, w_down):
    tok_rows, features = tokens.shape
    experts = lax.axis_size("z") * lax.axis_size("yl")
    cap = 3 * tok_rows // experts
    half = features // 2
    wg, wu, wd = w_gate[0], w_up[0], w_down[0]
    c = lax.axis_index("c")
    scal = jnp.stack([c] + [lax.axis_index(a) for a in ("x", "z", "yl")]).astype(jnp.int32)

    t_blocks, d_mine, placing, w_hi, w_lo = route(
        scal, expert_ids, gates, tokens, cotangent, experts, cap
    )
    d_mine = all_exchange(d_mine)

    wg2 = lax.dynamic_slice_in_dim(wg, (1 - c) * half, half, 0)
    wu2 = lax.dynamic_slice_in_dim(wu, (1 - c) * half, half, 0)
    wd2 = lax.dynamic_slice_in_dim(wd, (1 - c) * half, half, 1)
    d_mine, t_blocks, wg2, wu2, wd2 = lax.optimization_barrier((d_mine, t_blocks, wg2, wu2, wd2))
    wg2, wu2, wd2 = swap(wg2), swap(wu2), swap(wd2)

    d_own = gather_x(d_mine)
    t_own = exchange(t_blocks)
    t_oth = [swap(v) for v in t_own]
    d_chunks = d_own + [swap(v) for v in d_own]

    hid, silu, dsilu, routed = gate_up(scal, t_own, t_oth, wg, wu)
    hid2 = swap(hid)
    dgu = back_hidden(scal, d_chunks, wd, silu, dsilu)
    dgu2 = swap(dgu)

    out = out_half(scal, hid, hid2, wd, wd2)
    home = all_exchange(out)

    dgu, dgu2 = after((dgu, dgu2), out)
    parts, sent = {}, []
    for d in (2, 1, 3, 0):
        parts[d] = in_part(scal, d, dgu, dgu2, wg, wu, wg2, wu2)
        if d:
            sent.append(shift(parts[d], "x", d))
    home, parts[0] = lax.optimization_barrier((home, parts[0]))
    quarters = combine(scal, [w_hi, w_lo], home, True)
    m_sent = [shift(quarters[d], "x", d) for d in (2, 1, 3)]
    grad_down = grad_out(scal, after(hid, parts[0]), d_chunks)
    sent, grad_down = lax.optimization_barrier((sent, grad_down))
    g_home = add(scal, parts[0], *sent)
    grad_gate, grad_up = grad_in(scal, routed, after(dgu, g_home))
    g_home = all_exchange(g_home)
    g_home, grad_gate, grad_up = lax.optimization_barrier((g_home, grad_gate, grad_up))
    g_mine = combine(scal, [placing], g_home, False)[0]
    g_mine, m_sent = lax.optimization_barrier((g_mine, m_sent))
    token_grad = finish(scal, g_mine)
    mixed = finish(scal, add(scal, quarters[0], *m_sent))
    return (mixed, token_grad, grad_gate[None], grad_up[None], grad_down[None])


def solution(mesh):
    fine = Mesh(mesh.devices.reshape(4, 2, 2, 4, 2), ("z", "yl", "yh", "x", "c"))
    placed = (
        P(EXP, None),
        P(EXP, None),
        P(EXP, None),
        P(EXP, None),
        P(EXP, None, TEN),
        P(EXP, None, TEN),
        P(EXP, TEN, None),
    )
    return jax.shard_map(
        on_device,
        mesh=fine,
        in_specs=placed,
        out_specs=(
            P(EXP, None),
            P(EXP, None),
            P(EXP, None, TEN),
            P(EXP, None, TEN),
            P(EXP, TEN, None),
        ),
        check_vma=False,
    )
```

```python
import jax
import jax.numpy as jnp
from jax import lax
from jax.experimental import pallas as pl
from jax.experimental.pallas import tpu as pltpu
from jax.sharding import Mesh, PartitionSpec as P

F32, BF16 = jnp.float32, jnp.bfloat16
EXP = ("z", "yl")
TEN = ("yh", "x", "c")
NN = (((1,), (0,)), ((), ()))
NT = (((1,), (1,)), ((), ()))
TN = (((0,), (0,)), ((), ()))


def mm(a, b, dims=NN):
    return lax.dot_general(a, b, dims, preferred_element_type=F32)


def call(kernel, out_shape, grid, in_specs, out_specs, scratch=(), mib=24):
    return pl.pallas_call(
        kernel,
        out_shape=out_shape,
        grid_spec=pltpu.PrefetchScalarGridSpec(
            num_scalar_prefetch=1,
            grid=grid,
            in_specs=in_specs,
            out_specs=out_specs,
            scratch_shapes=list(scratch),
        ),
        compiler_params=pltpu.CompilerParams(vmem_limit_bytes=mib * 2**20),
        cost_estimate=pl.CostEstimate(flops=1, transcendentals=0, bytes_accessed=1),
    )


def shape(*dims, dtype=BF16):
    return jax.ShapeDtypeStruct(dims, dtype)


def in_hbm(*values):
    return [pltpu.with_memory_space_constraint(v, pltpu.HBM) for v in values]


def block(dims, index=None):
    return pl.BlockSpec(
        dims, index or (lambda *_: (0,) * len(dims)), pipeline_mode=pl.Buffered(1)
    )


def chunk_index(s, j):
    core = s[0] if j < 4 else 1 - s[0]
    return core * 4 + lax.rem(s[1] + j % 4, 4)


def route(scal, ids, gates, cotangent, experts, cap):
    toks, features = cotangent.shape
    part, slots = features // 8, experts * cap

    def kernel(s, ids_ref, gates_ref, cot_ref, moved_ref, place_ref, hi_ref, lo_ref):
        named = jnp.transpose(ids_ref[...])
        named0, named1 = named[:, 0:1], named[:, 1:2]
        lane = lax.broadcasted_iota(jnp.int32, (toks, 128), 1)
        onehot = ((named0 == lane) | (named1 == lane)).astype(F32).astype(BF16)
        row = lax.broadcasted_iota(jnp.int32, (toks, toks), 0)
        col = lax.broadcasted_iota(jnp.int32, (toks, toks), 1)
        earlier = (col < row).astype(F32).astype(BF16)
        count = mm(earlier, onehot).astype(BF16)
        ex = lax.broadcasted_iota(jnp.int32, (128, slots), 0) * cap
        at = lax.broadcasted_iota(jnp.int32, (128, slots), 1)
        spread = ((at >= ex) & (at < ex + cap)).astype(F32).astype(BF16)
        rank = mm(count, spread)
        slot = lax.broadcasted_iota(jnp.int32, (toks, slots), 1)
        first, second = named0 * cap, named1 * cap
        in0 = (slot >= first) & (slot < first + cap)
        in1 = (slot >= second) & (slot < second + cap)
        base = jnp.where(in0, first, jnp.where(in1, second, -4 * slots))
        hit = rank.astype(jnp.int32) + base == slot
        g = jnp.transpose(gates_ref[...])
        weight = jnp.where(hit, jnp.where(in0, g[:, 0:1], g[:, 1:2]), 0.0)
        hi = weight.astype(BF16)
        lo = (weight - hi.astype(F32)).astype(BF16)
        place_ref[...] = hit.astype(F32).astype(BF16)
        hi_ref[...] = hi
        lo_ref[...] = lo
        cot = cot_ref[...]
        moved_ref[...] = (mm(hi, cot, TN) + mm(lo, cot, TN)).astype(BF16)

    return call(
        kernel,
        [pltpu.HBM((slots, part), BF16), pltpu.VMEM((toks, slots), BF16)]
        + [pltpu.HBM((toks, slots), BF16)] * 2,
        (1,),
        [
            block(ids.shape[::-1]),
            block(gates.shape[::-1]),
            block((toks, part), lambda k, s: (0, s[0] * 4 + s[1])),
        ],
        [block((slots, part))] + [block((toks, slots))] * 3,
    )(scal, *in_hbm(ids.T, gates.T, cotangent))


def place(scal, placing, tokens):
    toks, slots = placing.shape
    half = tokens.shape[1] // 2

    def kernel(s, place_ref, tok_ref, out_ref):
        out_ref[...] = mm(place_ref[...], tok_ref[...], TN).astype(BF16)

    return call(
        kernel,
        pltpu.HBM((slots, half), BF16),
        (3,),
        [
            block((toks, slots)),
            pl.BlockSpec((toks, half // 3), lambda k, s: (0, s[0] * 3 + k)),
        ],
        pl.BlockSpec((slots, half // 3), lambda k, s: (0, k)),
        mib=12,
    )(scal, placing, *in_hbm(tokens))


def gate_up(scal, t_half, wg, wu, sums):
    rows, half = t_half.shape
    ff = wg.shape[1]
    rb = rows // 3
    last = sums is not None

    def kernel(s, t_ref, wg_ref, wu_ref, *refs):
        left = t_ref[...]
        gate, up = mm(left, wg_ref[...]), mm(left, wu_ref[...])
        if not last:
            refs[0][...], refs[1][...] = gate, up
            return
        gate, up = gate + refs[0][...], up + refs[1][...]
        sig = jax.nn.sigmoid(gate)
        silu = gate * sig
        refs[2][...] = (silu * up).astype(BF16)
        refs[3][...] = silu
        refs[4][...] = up * sig * (1.0 + gate * (1.0 - sig))

    rows_of = pl.BlockSpec((rb, ff), lambda k, s: (k, 0))
    weights = block((half, ff), lambda k, s: ((1 - s[0]) if last else s[0], 0))
    wide = pltpu.VMEM((rows, ff), F32)
    return call(
        kernel,
        [pltpu.VMEM((rows, ff), BF16), wide, wide] if last else [wide, wide],
        (3,),
        [pl.BlockSpec((rb, half), lambda k, s: (k, 0)), weights, weights]
        + ([rows_of] * 2 if last else []),
        [rows_of] * (3 if last else 2),
        mib=20,
    )(scal, *in_hbm(t_half, wg, wu), *(sums or ()))


def back_hidden(scal, chunks, wd, sums):
    rows, cols = chunks[0].shape
    ff = wd.shape[0]
    rb = rows
    last = sums is not None

    def kernel(s, c0, c1, c2, c3, wd_ref, *refs):
        acc = refs[0][...] if last else None
        for j, ref in enumerate((c0, c1, c2, c3)):
            at = pl.multiple_of(lax.rem(s[1] + j, 4) * cols, 128)
            part = mm(ref[...], wd_ref[:, pl.ds(at, cols)], NT)
            acc = part if acc is None else acc + part
        if not last:
            refs[0][...] = acc
            return
        refs[3][:, :ff] = (acc * refs[2][...]).astype(BF16)
        refs[3][:, ff:] = (acc * refs[1][...]).astype(BF16)

    rows_of = block((rb, ff))
    return call(
        kernel,
        pltpu.VMEM((rows, 2 * ff), BF16) if last else pltpu.VMEM((rows, ff), F32),
        (1,),
        [block((rb, cols))] * 4
        + [block((ff, 4 * cols), lambda k, s: (0, (1 - s[0]) if last else s[0]))]
        + ([rows_of] * 3 if last else []),
        block((rb, 2 * ff)) if last else rows_of,
        mib=20,
    )(scal, *chunks, *in_hbm(wd), *(sums or ()))


def in_part(scal, steps, mine, theirs, wg, wu, wgu2):
    rows, ff = mine.shape[0], mine.shape[1] // 2
    cols = wgu2.shape[0] // 8

    def kernel(s, m, t, *refs):
        weights = [
            jnp.concatenate([refs[2 * k][...], refs[2 * k + 1][...]], axis=0) for k in range(4)
        ]
        acc = mm(m[:, :ff], weights[0], NT) + mm(m[:, ff:], weights[1], NT)
        acc += mm(t[:, :ff], weights[2], NT) + mm(t[:, ff:], weights[3], NT)
        for k in range(2):
            refs[8 + k][...] = acc[:, k * cols : (k + 1) * cols].astype(BF16)

    here = [block((cols, ff), lambda k, s, d=d: (s[0] * 4 + lax.rem(s[1] + d, 4), 0)) for d in steps]
    there = [
        block((cols, ff), lambda k, s, d=d, b=b: (b + lax.rem(s[1] + d, 4), 0))
        for b in (0, 4)
        for d in steps
    ]
    return call(
        kernel,
        [pltpu.HBM((rows, cols), BF16)] * 2,
        (1,),
        [block((rows, 2 * ff))] * 2 + here * 2 + there,
        [block((rows, cols))] * 2,
        mib=20,
    )(scal, mine, theirs, *in_hbm(wg, wg, wu, wu, *[wgu2] * 4))


def out_half(scal, hid, hid2, wd, wd2):
    rows, ff = hid.shape
    half = wd2.shape[1]
    cols = half // 2

    def kernel(s, h0, h1, w0, w1, out):
        out[...] = (mm(h0[...], w0[...]) + mm(h1[...], w1[...])).astype(BF16)

    return call(
        kernel,
        pltpu.HBM((rows, half), BF16),
        (2,),
        [
            block((rows, ff)),
            block((rows, ff)),
            pl.BlockSpec((ff, cols), lambda k, s: (0, s[0] * 2 + k)),
            pl.BlockSpec((ff, cols), lambda k, s: (0, k)),
        ],
        pl.BlockSpec((rows, cols), lambda k, s: (0, k)),
        mib=16,
    )(scal, hid, hid2, *in_hbm(wd, wd2))


def add(scal, *parts):
    rows, cols = parts[0].shape
    rb = rows // 4 if rows > 256 else rows

    def kernel(s, *refs):
        acc = refs[0][...].astype(F32)
        for ref in refs[1:-1]:
            acc = acc + ref[...].astype(F32)
        refs[-1][...] = acc.astype(BF16)

    rows_of = pl.BlockSpec((rb, cols), lambda k, s: (k, 0))
    return call(
        kernel,
        shape(rows, cols),
        (rows // rb,),
        [rows_of] * len(parts),
        rows_of,
        mib=8,
    )(scal, *parts)


def combine(scal, mats, home, quarters):
    toks, slots = mats[0].shape
    cols = home.shape[1]
    n = len(mats)

    def kernel(s, *refs):
        mat_refs, home_ref, rest = refs[:n], refs[n], refs[n + 1 :]
        acc = mm(mat_refs[0][...], home_ref[...])
        for m in mat_refs[1:]:
            acc += mm(m[...], home_ref[...])
        if quarters:
            whole = rest[-1]
            whole[...] = acc
            for d in range(4):
                at = pl.multiple_of(lax.rem(s[1] + d, 4) * (cols // 4), 128)
                rest[d][...] = whole[:, pl.ds(at, cols // 4)].astype(BF16)
        else:
            rest[0][...] = acc.astype(BF16)

    if quarters:
        dims, k, extra = (toks, cols // 4), 4, [pltpu.VMEM((toks, cols), F32)]
    else:
        dims, k, extra = (toks, cols), 1, []
    return call(
        kernel,
        [shape(*dims)] * k,
        (1,),
        [block((toks, slots))] * n + [block((slots, cols))],
        [block(dims)] * k,
        extra,
        mib=12,
    )(scal, *mats, home)


def grad_in(scal, own, oth, dgu):
    rows, half = own.shape
    ff = dgu.shape[1] // 2
    kb = half // 2

    def kernel(s, own_ref, oth_ref, dgu_ref, gg_ref, gu_ref):
        def put(left_ref):
            res = mm(left_ref[...], dgu_ref[...], TN).astype(BF16)
            gg_ref[...] = res[:, :ff]
            gu_ref[...] = res[:, ff:]

        k = pl.program_id(0)
        pl.when(k < 2)(lambda: put(own_ref))
        pl.when(k >= 2)(lambda: put(oth_ref))

    def place_of(k, s):
        return (jnp.where(k < 2, s[0], 1 - s[0]) * 2 + k % 2, 0)

    return call(
        kernel,
        [pltpu.HBM((2 * half, ff), BF16)] * 2,
        (4,),
        [
            pl.BlockSpec((rows, kb), lambda k, s: (0, jnp.minimum(k, 1))),
            pl.BlockSpec((rows, kb), lambda k, s: (0, jnp.maximum(k - 2, 0))),
            block(dgu.shape),
        ],
        [pl.BlockSpec((kb, ff), place_of)] * 2,
        mib=20,
    )(scal, *in_hbm(own, oth), dgu)


def grad_out(scal, hid, chunks):
    rows, cols = chunks[0].shape
    ff = hid.shape[1]

    def kernel(s, hid_ref, *refs):
        for j in range(8):
            at = pl.multiple_of(chunk_index(s, j) * cols, 128)
            refs[8][:, pl.ds(at, cols)] = mm(hid_ref[...], refs[j][...], TN).astype(BF16)

    return call(
        kernel,
        pltpu.HBM((ff, 8 * cols), BF16),
        (1,),
        [block((rows, ff))] + [block((rows, cols))] * 8,
        block((ff, 8 * cols)),
        mib=20,
    )(scal, hid, *chunks)


def assemble(scal, chunks):
    rows, cols = chunks[0].shape

    def kernel(s, *refs):
        for j in range(8):
            at = pl.multiple_of(chunk_index(s, j) * cols, 128)
            refs[8][:, pl.ds(at, cols)] = refs[j][...]

    return call(
        kernel,
        shape(rows, 8 * cols),
        (1,),
        [block((rows, cols))] * 8,
        block((rows, 8 * cols)),
        mib=8,
    )(scal, *chunks)


def swap(v, axis="c"):
    return lax.ppermute(v, axis, [(0, 1), (1, 0)])


def shift(v, axis, d):
    n = lax.axis_size(axis)
    return lax.ppermute(v, axis, [(i, (i + d) % n) for i in range(n)])


def all_exchange(rows):
    cut = rows.reshape(8, rows.shape[0] // 8, rows.shape[1])
    return lax.all_to_all(cut, EXP, split_axis=0, concat_axis=0, tiled=True).reshape(rows.shape)


def to_q(v, d, over_y):
    return swap(v, "yh") if d == 2 and over_y else shift(v, "x", d)


def gather_q(v, over_y):
    far, right, left = to_q(v, 2, over_y), to_q(v, 3, over_y), to_q(v, 1, over_y)
    return [v, right, far, left]


def after(value, *earlier):
    return lax.optimization_barrier((value, earlier))[0]


def finish(scal, mine):
    other = [(yh * 4 + x, (1 - yh) * 4 + (x + 2) % 4) for yh in range(2) for x in range(4)]
    total = add(scal, mine, lax.ppermute(mine, ("yh", "x"), other))
    chunks = gather_q(total, True)
    return assemble(scal, chunks + [swap(v) for v in chunks])


def on_device(tokens, cotangent, expert_ids, gates, w_gate, w_up, w_down):
    tok_rows, features = tokens.shape
    experts = lax.axis_size("z") * lax.axis_size("yl")
    cap = 3 * tok_rows // experts
    half = features // 2
    wg, wu, wd = w_gate[0], w_up[0], w_down[0]
    c = lax.axis_index("c")
    q = lax.rem(lax.axis_index("x") + 2 * lax.axis_index("yh"), 4)
    scal = jnp.stack([c, q]).astype(jnp.int32)

    d_mine, placing, w_hi, w_lo = route(scal, expert_ids, gates, cotangent, experts, cap)
    d_mine = all_exchange(d_mine)

    t_rows = place(scal, placing, tokens)
    wgu2 = jnp.concatenate(
        [lax.dynamic_slice_in_dim(w, (1 - c) * half, half, 0) for w in (wg, wu)], axis=0
    )
    wd2 = lax.dynamic_slice_in_dim(wd, (1 - c) * half, half, 1)
    d_mine, t_rows, wgu2, wd2 = lax.optimization_barrier((d_mine, t_rows, wgu2, wd2))

    t_own = all_exchange(t_rows)
    d_own = gather_q(d_mine, False)
    wgu2, wd2 = swap(wgu2), swap(wd2)
    t_own, d_own, wgu2, wd2 = lax.optimization_barrier((t_own, d_own, wgu2, wd2))
    t_oth = swap(t_own)
    d_oth = [swap(v) for v in d_own]

    sums = gate_up(scal, t_own, wg, wu, None)
    d_sum = back_hidden(scal, d_own, wd, None)
    hid, silu, dsilu = gate_up(scal, t_oth, wg, wu, sums)
    hid2 = swap(hid)
    dgu = back_hidden(scal, d_oth, wd, (d_sum, silu, dsilu))
    dgu2 = swap(dgu)

    out = out_half(scal, hid, hid2, wd, wd2)
    home = all_exchange(out)

    dgu, dgu2 = after((dgu, dgu2), out)
    parts, sent = {}, {}
    parts[2], parts[1] = in_part(scal, (2, 1), dgu, dgu2, wg, wu, wgu2)
    sent[2], sent[1] = to_q(parts[2], 2, False), to_q(parts[1], 1, False)
    dgu = after(dgu, parts[1])
    parts[3], parts[0] = in_part(scal, (3, 0), dgu, dgu2, wg, wu, wgu2)
    sent[3] = to_q(parts[3], 3, False)
    dgu, hid = after((dgu, hid), parts[0])
    grad_gate, grad_up = grad_in(scal, t_own, t_oth, dgu)
    hid, sent[2], sent[1] = after((hid, sent[2], sent[1]), grad_up)
    hid = after(hid, sent[2], sent[1])
    grad_down = grad_out(scal, hid, d_own + d_oth)
    sent, home, grad_gate, grad_up, grad_down = lax.optimization_barrier(
        (sent, home, grad_gate, grad_up, grad_down)
    )
    g_home = add(scal, parts[0], sent[2], sent[1], sent[3])
    quarters = combine(scal, [w_hi, w_lo], home, True)
    g_home = all_exchange(g_home)
    m_sent = [to_q(quarters[d], d, True) for d in (2, 1, 3)]
    g_mine = combine(scal, [placing], g_home, False)[0]
    m_sent = after(m_sent, g_mine)
    token_grad = finish(scal, g_mine)
    mixed = finish(scal, add(scal, quarters[0], *m_sent))
    return (mixed, token_grad, grad_gate[None], grad_up[None], grad_down[None])


def solution(mesh):
    fine = Mesh(mesh.devices.reshape(4, 2, 2, 4, 2), ("z", "yl", "yh", "x", "c"))
    placed = (
        P(EXP, None),
        P(EXP, None),
        P(EXP, None),
        P(EXP, None),
        P(EXP, None, TEN),
        P(EXP, None, TEN),
        P(EXP, TEN, None),
    )
    return jax.shard_map(
        on_device,
        mesh=fine,
        in_specs=placed,
        out_specs=(
            P(EXP, None),
            P(EXP, None),
            P(EXP, None, TEN),
            P(EXP, None, TEN),
            P(EXP, TEN, None),
        ),
        check_vma=False,
    )
```

```python
import jax
import jax.numpy as jnp
from jax import lax
from jax.experimental import pallas as pl
from jax.experimental.pallas import tpu as pltpu
from jax.sharding import Mesh, PartitionSpec as P

F32, BF16 = jnp.float32, jnp.bfloat16
EXP = ("z", "yl")
TEN = ("yh", "x", "c")
NN = (((1,), (0,)), ((), ()))
NT = (((1,), (1,)), ((), ()))
TN = (((0,), (0,)), ((), ()))


def mm(a, b, dims=NN):
    return lax.dot_general(a, b, dims, preferred_element_type=F32)


def call(kernel, out_shape, grid, in_specs, out_specs, scratch=(), mib=24):
    return pl.pallas_call(
        kernel,
        out_shape=out_shape,
        grid_spec=pltpu.PrefetchScalarGridSpec(
            num_scalar_prefetch=1,
            grid=grid,
            in_specs=in_specs,
            out_specs=out_specs,
            scratch_shapes=list(scratch),
        ),
        compiler_params=pltpu.CompilerParams(vmem_limit_bytes=mib * 2**20),
        cost_estimate=pl.CostEstimate(flops=1, transcendentals=0, bytes_accessed=1),
    )


def shape(*dims, dtype=BF16):
    return jax.ShapeDtypeStruct(dims, dtype)


def in_hbm(*values):
    return [pltpu.with_memory_space_constraint(v, pltpu.HBM) for v in values]


def block(dims, index=None):
    return pl.BlockSpec(
        dims, index or (lambda *_: (0,) * len(dims)), pipeline_mode=pl.Buffered(1)
    )


def chunk_index(s, j):
    core = s[0] if j < 4 else 1 - s[0]
    return core * 4 + lax.rem(s[1] + j % 4, 4)


def route(scal, ids, gates, cotangent, experts, cap):
    toks, features = cotangent.shape
    part, slots = features // 8, experts * cap

    def kernel(s, ids_ref, gates_ref, cot_ref, moved_ref, place_ref, hi_ref, lo_ref):
        named = jnp.transpose(ids_ref[...])
        named0, named1 = named[:, 0:1], named[:, 1:2]
        lane = lax.broadcasted_iota(jnp.int32, (toks, 128), 1)
        onehot = ((named0 == lane) | (named1 == lane)).astype(F32).astype(BF16)
        row = lax.broadcasted_iota(jnp.int32, (toks, toks), 0)
        col = lax.broadcasted_iota(jnp.int32, (toks, toks), 1)
        earlier = (col < row).astype(F32).astype(BF16)
        count = mm(earlier, onehot).astype(BF16)
        ex = lax.broadcasted_iota(jnp.int32, (128, slots), 0) * cap
        at = lax.broadcasted_iota(jnp.int32, (128, slots), 1)
        spread = ((at >= ex) & (at < ex + cap)).astype(F32).astype(BF16)
        rank = mm(count, spread)
        slot = lax.broadcasted_iota(jnp.int32, (toks, slots), 1)
        first, second = named0 * cap, named1 * cap
        in0 = (slot >= first) & (slot < first + cap)
        in1 = (slot >= second) & (slot < second + cap)
        base = jnp.where(in0, first, jnp.where(in1, second, -4 * slots))
        hit = rank.astype(jnp.int32) + base == slot
        g = jnp.transpose(gates_ref[...])
        weight = jnp.where(hit, jnp.where(in0, g[:, 0:1], g[:, 1:2]), 0.0)
        hi = weight.astype(BF16)
        lo = (weight - hi.astype(F32)).astype(BF16)
        place_ref[...] = hit.astype(F32).astype(BF16)
        hi_ref[...] = hi
        lo_ref[...] = lo
        cot = cot_ref[...]
        moved_ref[...] = (mm(hi, cot, TN) + mm(lo, cot, TN)).astype(BF16)

    return call(
        kernel,
        [pltpu.HBM((slots, part), BF16), pltpu.VMEM((toks, slots), BF16)]
        + [pltpu.HBM((toks, slots), BF16)] * 2,
        (1,),
        [
            block(ids.shape[::-1]),
            block(gates.shape[::-1]),
            block((toks, part), lambda k, s: (0, s[0] * 4 + s[1])),
        ],
        [block((slots, part))] + [block((toks, slots))] * 3,
    )(scal, *in_hbm(ids.T, gates.T, cotangent))


def place(scal, placing, tokens):
    toks, slots = placing.shape
    half = tokens.shape[1] // 2

    def kernel(s, place_ref, tok_ref, out_ref):
        out_ref[...] = mm(place_ref[...], tok_ref[...], TN).astype(BF16)

    return call(
        kernel,
        pltpu.HBM((slots, half), BF16),
        (3,),
        [
            block((toks, slots)),
            pl.BlockSpec((toks, half // 3), lambda k, s: (0, s[0] * 3 + k)),
        ],
        pl.BlockSpec((slots, half // 3), lambda k, s: (0, k)),
        mib=12,
    )(scal, placing, *in_hbm(tokens))


def gate_up(scal, t_half, wg, wu, sums):
    rows, half = t_half.shape
    ff = wg.shape[1]
    rb = rows // 3
    last = sums is not None

    def kernel(s, t_ref, wg_ref, wu_ref, *refs):
        left = t_ref[...]
        gate, up = mm(left, wg_ref[...]), mm(left, wu_ref[...])
        if not last:
            refs[0][...], refs[1][...] = gate, up
            return
        gate, up = gate + refs[0][...], up + refs[1][...]
        sig = jax.nn.sigmoid(gate)
        silu = gate * sig
        refs[2][...] = (silu * up).astype(BF16)
        refs[3][...] = silu
        refs[4][...] = up * sig * (1.0 + gate * (1.0 - sig))

    rows_of = pl.BlockSpec((rb, ff), lambda k, s: (k, 0))
    weights = block((half, ff), lambda k, s: ((1 - s[0]) if last else s[0], 0))
    wide = pltpu.VMEM((rows, ff), F32)
    return call(
        kernel,
        [pltpu.VMEM((rows, ff), BF16), wide, wide] if last else [wide, wide],
        (3,),
        [pl.BlockSpec((rb, half), lambda k, s: (k, 0)), weights, weights]
        + ([rows_of] * 2 if last else []),
        [rows_of] * (3 if last else 2),
        mib=20,
    )(scal, *([t_half] if last else in_hbm(t_half)), *in_hbm(wg, wu), *(sums or ()))


def back_hidden(scal, chunks, wd, sums):
    rows, cols = chunks[0].shape
    ff = wd.shape[0]
    rb = rows
    last = sums is not None

    def kernel(s, c0, c1, c2, c3, wd_ref, *refs):
        acc = refs[0][...] if last else None
        for j, ref in enumerate((c0, c1, c2, c3)):
            at = pl.multiple_of(lax.rem(s[1] + j, 4) * cols, 128)
            part = mm(ref[...], wd_ref[:, pl.ds(at, cols)], NT)
            acc = part if acc is None else acc + part
        if not last:
            refs[0][...] = acc
            return
        refs[3][:, :ff] = (acc * refs[2][...]).astype(BF16)
        refs[3][:, ff:] = (acc * refs[1][...]).astype(BF16)

    rows_of = block((rb, ff))
    return call(
        kernel,
        pltpu.VMEM((rows, 2 * ff), BF16) if last else pltpu.VMEM((rows, ff), F32),
        (1,),
        [block((rb, cols))] * 4
        + [block((ff, 4 * cols), lambda k, s: (0, (1 - s[0]) if last else s[0]))]
        + ([rows_of] * 3 if last else []),
        block((rb, 2 * ff)) if last else rows_of,
        mib=20,
    )(scal, *chunks, *in_hbm(wd), *(sums or ()))


def in_part(scal, steps, mine, theirs, wg, wu, wgu2):
    rows, ff = mine.shape[0], mine.shape[1] // 2
    cols = wgu2.shape[0] // 8

    def kernel(s, m, t, *refs):
        weights = [
            jnp.concatenate([refs[2 * k][...], refs[2 * k + 1][...]], axis=0) for k in range(4)
        ]
        acc = mm(m[:, :ff], weights[0], NT) + mm(m[:, ff:], weights[1], NT)
        acc += mm(t[:, :ff], weights[2], NT) + mm(t[:, ff:], weights[3], NT)
        for k in range(2):
            refs[8 + k][...] = acc[:, k * cols : (k + 1) * cols].astype(BF16)

    here = [block((cols, ff), lambda k, s, d=d: (s[0] * 4 + lax.rem(s[1] + d, 4), 0)) for d in steps]
    there = [
        block((cols, ff), lambda k, s, d=d, b=b: (b + lax.rem(s[1] + d, 4), 0))
        for b in (0, 4)
        for d in steps
    ]
    return call(
        kernel,
        [pltpu.HBM((rows, cols), BF16)] * 2,
        (1,),
        [block((rows, 2 * ff))] * 2 + here * 2 + there,
        [block((rows, cols))] * 2,
        mib=20,
    )(scal, mine, theirs, *in_hbm(wg, wg, wu, wu, *[wgu2] * 4))


def out_half(scal, hid, hid2, wd, wd2):
    rows, ff = hid.shape
    half = wd2.shape[1]
    cols = half // 2

    def kernel(s, h0, h1, w0, w1, out):
        out[...] = (mm(h0[...], w0[...]) + mm(h1[...], w1[...])).astype(BF16)

    return call(
        kernel,
        pltpu.HBM((rows, half), BF16),
        (2,),
        [
            block((rows, ff)),
            block((rows, ff)),
            pl.BlockSpec((ff, cols), lambda k, s: (0, s[0] * 2 + k)),
            pl.BlockSpec((ff, cols), lambda k, s: (0, k)),
        ],
        pl.BlockSpec((rows, cols), lambda k, s: (0, k)),
        mib=16,
    )(scal, hid, hid2, *in_hbm(wd, wd2))


def add(scal, *parts):
    rows, cols = parts[0].shape
    rb = rows // 2 if rows > 256 else rows

    def kernel(s, *refs):
        acc = refs[0][...].astype(F32)
        for ref in refs[1:-1]:
            acc = acc + ref[...].astype(F32)
        refs[-1][...] = acc.astype(BF16)

    rows_of = pl.BlockSpec((rb, cols), lambda k, s: (k, 0))
    return call(
        kernel,
        shape(rows, cols),
        (rows // rb,),
        [rows_of] * len(parts),
        rows_of,
        mib=8,
    )(scal, *parts)


def combine(scal, mats, home, quarters):
    toks, slots = mats[0].shape
    cols = home.shape[1]
    n = len(mats)

    def kernel(s, *refs):
        mat_refs, home_ref, rest = refs[:n], refs[n], refs[n + 1 :]
        acc = mm(mat_refs[0][...], home_ref[...])
        for m in mat_refs[1:]:
            acc += mm(m[...], home_ref[...])
        if quarters:
            whole = rest[-1]
            whole[...] = acc
            for d in range(4):
                at = pl.multiple_of(lax.rem(s[1] + d, 4) * (cols // 4), 128)
                rest[d][...] = whole[:, pl.ds(at, cols // 4)].astype(BF16)
        else:
            rest[0][...] = acc.astype(BF16)

    if quarters:
        dims, k, extra = (toks, cols // 4), 4, [pltpu.VMEM((toks, cols), F32)]
    else:
        dims, k, extra = (toks, cols), 1, []
    return call(
        kernel,
        [shape(*dims)] * k,
        (1,),
        [block((toks, slots))] * n + [block((slots, cols))],
        [block(dims)] * k,
        extra,
        mib=12,
    )(scal, *mats, home)


def grad_in(scal, own, oth, dgu):
    rows, half = own.shape
    ff = dgu.shape[1] // 2
    kb = half // 2

    def kernel(s, own_ref, oth_ref, dgu_ref, gg_ref, gu_ref):
        def put(left_ref):
            res = mm(left_ref[...], dgu_ref[...], TN).astype(BF16)
            gg_ref[...] = res[:, :ff]
            gu_ref[...] = res[:, ff:]

        k = pl.program_id(0)
        pl.when(k < 2)(lambda: put(own_ref))
        pl.when(k >= 2)(lambda: put(oth_ref))

    def place_of(k, s):
        return (jnp.where(k < 2, s[0], 1 - s[0]) * 2 + k % 2, 0)

    return call(
        kernel,
        [pltpu.HBM((2 * half, ff), BF16)] * 2,
        (4,),
        [
            pl.BlockSpec((rows, kb), lambda k, s: (0, jnp.minimum(k, 1))),
            pl.BlockSpec((rows, kb), lambda k, s: (0, jnp.maximum(k - 2, 0))),
            block(dgu.shape),
        ],
        [pl.BlockSpec((kb, ff), place_of)] * 2,
        mib=20,
    )(scal, *in_hbm(own), oth, dgu)


def grad_out(scal, hid, chunks):
    rows, cols = chunks[0].shape
    ff = hid.shape[1]

    def kernel(s, hid_ref, *refs):
        for j in range(8):
            at = pl.multiple_of(chunk_index(s, j) * cols, 128)
            refs[8][:, pl.ds(at, cols)] = mm(hid_ref[...], refs[j][...], TN).astype(BF16)

    return call(
        kernel,
        pltpu.HBM((ff, 8 * cols), BF16),
        (1,),
        [block((rows, ff))] + [block((rows, cols))] * 8,
        block((ff, 8 * cols)),
        mib=20,
    )(scal, hid, *chunks)


def assemble(scal, *lists):
    rows, cols = lists[0][0].shape
    n, rb = len(lists), rows // 4

    def kernel(s, *refs):
        for i in range(n):
            for j in range(8):
                at = pl.multiple_of(chunk_index(s, j) * cols, 128)
                refs[8 * n + i][:, pl.ds(at, cols)] = refs[8 * i + j][...]

    rows_of = lambda k, s: (k, 0)
    return call(
        kernel,
        [pltpu.HBM((rows, 8 * cols), BF16)] * n,
        (4,),
        [pl.BlockSpec((rb, cols), rows_of)] * (8 * n),
        [pl.BlockSpec((rb, 8 * cols), rows_of)] * n,
        mib=12,
    )(scal, *[v for chunks in lists for v in chunks])


def swap(v, axis="c"):
    return lax.ppermute(v, axis, [(0, 1), (1, 0)])


def shift(v, axis, d):
    n = lax.axis_size(axis)
    return lax.ppermute(v, axis, [(i, (i + d) % n) for i in range(n)])


def all_exchange(rows):
    cut = rows.reshape(8, rows.shape[0] // 8, rows.shape[1])
    return lax.all_to_all(cut, EXP, split_axis=0, concat_axis=0, tiled=True).reshape(rows.shape)


def to_q(v, d, over_y):
    return swap(v, "yh") if d == 2 and over_y else shift(v, "x", d)


def gather_q(v, over_y):
    far, right, left = to_q(v, 2, over_y), to_q(v, 3, over_y), to_q(v, 1, over_y)
    return [v, right, far, left]


def after(value, *earlier):
    return lax.optimization_barrier((value, earlier))[0]


def finish(scal, mine):
    other = [(yh * 4 + x, (1 - yh) * 4 + (x + 2) % 4) for yh in range(2) for x in range(4)]
    total = add(scal, mine, lax.ppermute(mine, ("yh", "x"), other))
    chunks = gather_q(total, True)
    return chunks + [swap(v) for v in chunks]


def on_device(tokens, cotangent, expert_ids, gates, w_gate, w_up, w_down):
    tok_rows, features = tokens.shape
    experts = lax.axis_size("z") * lax.axis_size("yl")
    cap = 3 * tok_rows // experts
    half = features // 2
    wg, wu, wd = w_gate[0], w_up[0], w_down[0]
    c = lax.axis_index("c")
    q = lax.rem(lax.axis_index("x") + 2 * lax.axis_index("yh"), 4)
    scal = jnp.stack([c, q]).astype(jnp.int32)

    d_mine, placing, w_hi, w_lo = route(scal, expert_ids, gates, cotangent, experts, cap)
    d_mine = all_exchange(d_mine)

    t_rows = place(scal, placing, tokens)
    wgu2 = jnp.concatenate(
        [lax.dynamic_slice_in_dim(w, (1 - c) * half, half, 0) for w in (wg, wu)], axis=0
    )
    wd2 = lax.dynamic_slice_in_dim(wd, (1 - c) * half, half, 1)
    d_mine, t_rows, wgu2, wd2 = lax.optimization_barrier((d_mine, t_rows, wgu2, wd2))

    t_own = all_exchange(t_rows)
    d_own = gather_q(d_mine, False)
    wgu2, wd2 = swap(wgu2), swap(wd2)
    t_own, d_own, wgu2, wd2 = lax.optimization_barrier((t_own, d_own, wgu2, wd2))
    t_oth = swap(t_own)
    d_oth = [swap(v) for v in d_own]

    sums = gate_up(scal, t_own, wg, wu, None)
    d_sum = back_hidden(scal, d_own, wd, None)
    hid, silu, dsilu = gate_up(scal, t_oth, wg, wu, sums)
    hid2 = swap(hid)
    dgu = back_hidden(scal, d_oth, wd, (d_sum, silu, dsilu))
    dgu2 = swap(dgu)

    out = out_half(scal, hid, hid2, wd, wd2)
    home = all_exchange(out)

    dgu, dgu2 = after((dgu, dgu2), out)
    parts, sent = {}, {}
    parts[2], parts[1] = in_part(scal, (2, 1), dgu, dgu2, wg, wu, wgu2)
    sent[2], sent[1] = to_q(parts[2], 2, False), to_q(parts[1], 1, False)
    dgu = after(dgu, parts[1])
    parts[3], parts[0] = in_part(scal, (3, 0), dgu, dgu2, wg, wu, wgu2)
    sent[3] = to_q(parts[3], 3, False)
    dgu, hid = after((dgu, hid), parts[0])
    grad_gate, grad_up = grad_in(scal, t_own, t_oth, dgu)
    grad_down = grad_out(scal, after(hid, grad_up), d_own + d_oth)
    home, sent[2], sent[1], grad_down = lax.optimization_barrier(
        (home, sent[2], sent[1], grad_down)
    )
    quarters = combine(scal, [w_hi, w_lo], home, True)
    m_sent = [to_q(quarters[d], d, True) for d in (2, 1, 3)]
    sent = after(sent, quarters)
    g_home = all_exchange(add(scal, *in_hbm(parts[0], sent[2], sent[1]), sent[3]))
    g_mine = combine(scal, [placing], g_home, False)[0]
    m_sent = after(m_sent, g_mine)
    g_chunks = finish(scal, g_mine)
    m_chunks = finish(scal, add(scal, quarters[0], *m_sent))
    mixed, token_grad = assemble(scal, m_chunks, g_chunks)
    return (mixed, token_grad, grad_gate[None], grad_up[None], grad_down[None])


def solution(mesh):
    fine = Mesh(mesh.devices.reshape(4, 2, 2, 4, 2), ("z", "yl", "yh", "x", "c"))
    placed = (
        P(EXP, None),
        P(EXP, None),
        P(EXP, None),
        P(EXP, None),
        P(EXP, None, TEN),
        P(EXP, None, TEN),
        P(EXP, TEN, None),
    )
    return jax.shard_map(
        on_device,
        mesh=fine,
        in_specs=placed,
        out_specs=(
            P(EXP, None),
            P(EXP, None),
            P(EXP, None, TEN),
            P(EXP, None, TEN),
            P(EXP, TEN, None),
        ),
        check_vma=False,
    )
```
